256 devices in a mesh: gossip: 16 (over z, x_hi), shard: 16 (over y, x_lo, core).
Axes of the slice: x: 4 (x_hi: 2, x_lo: 2; x = x_hi * 2 + x_lo), y: 4, z: 8, core: 2. Of those that a mesh axis runs over, the one named last changes fastest.
Arguments:
- activations: bfloat16 [16, 2048, 2560], P('gossip', 'shard'), may hold values from -6 to 6
- out_grads: bfloat16 [16, 2048, 6912], P('gossip', 'shard'), may hold values from -0.13183594 to 0.13183594
- params: bfloat16 [16, 2560, 6912], P('gossip', 'shard'), may hold values from -6 to 6
- first_moment: bfloat16 [16, 2560, 6912], P('gossip', 'shard'), may hold values from -3 to 3
- second_moment: bfloat16 [16, 2560, 6912], P('gossip', 'shard'), may hold values from 0.0009994507 to 0.099609375
- gossip_round: int32 [1], replicated, may hold values from 0 to 2
- step_count: int32 [1], replicated, may hold values from 1 to 8
Outputs:
- averaged: bfloat16 [16, 2560, 6912], P('gossip', 'shard')
- new_moment: bfloat16 [16, 2560, 6912], P('gossip', 'shard')
The draws below stay inside these ranges and needn't reach their ends.
All inputs are finite; a program needn't handle non-finite values.
Results may differ from the reference program's by a relative error of at most 0.001.
The reference program's roundings to bfloat16 on the way (of `stepped`) count: a program that leaves them out, or rounds other values in their place, can miss the bound.
Values may be sent and summed in bfloat16 or wider, within the bound.
No kernel may reach another device: no remote copies, remote signals or barrier semaphores. Data moves between devices by JAX's collectives and lax.ppermute only.
A program may use at most 128 MiB of HBM per device.

```python
import math
import jax
import jax.numpy as jnp
from jax import lax

D = 2560
FF = 6912
ROUNDS = 3
REPLICAS = 16
TOKENS = 2048


def block_levels(stream_key, extent, pieces, least, largest):
    def one(position, blocks):
        steps = jax.random.uniform(jax.random.fold_in(jax.random.fold_in(stream_key, 6), position), (blocks,), jnp.float32, least / len(pieces), largest / len(pieces))
        return jnp.repeat(jnp.exp(steps), extent[position] // blocks).reshape((-1,) + (1,) * (len(extent) - position - 1))

    level = one(*pieces[0])
    for cut in pieces[1:]:
        level = level * one(*cut)
    return level


def centred(own_key, extent, deviation, reach, split=(), held_as=jnp.bfloat16):
    entries = jax.random.normal(own_key, extent, jnp.float32) * deviation
    if len(split) > 0:
        entries = block_levels(own_key, extent, split, -0.22, 0.18) * entries
    return jnp.clip(entries, min=-reach, max=reach).astype(held_as)


def setup_inputs(seed: int = 0) -> dict:
    key_of = jax.random.split(jax.random.key(seed), 8)
    activations = centred(key_of[0], (REPLICAS, TOKENS, D), 1.0, 6.0, ((0, 16), (1, 16)))
    out_grads = centred(key_of[1], (REPLICAS, TOKENS, FF), (1.0 / TOKENS ** 0.5), 0.13183594, ((0, 16), (1, 16)))
    params = centred(key_of[2], (REPLICAS, D, FF), 1.0, 6.0, ((0, 16), (1, 16)))
    first_moment = centred(key_of[3], (REPLICAS, D, FF), 0.5, 3.0, ((0, 16), (1, 16)))
    second_moment = jnp.clip(jnp.exp(math.log(0.099609375) - 4.6018058 * jax.random.uniform(key_of[4], (REPLICAS, D, FF), jnp.float32) ** block_levels(key_of[4], (REPLICAS, D, FF), ((0, 16), (1, 16)), -0.2, 0.2)), 0.0009994507, 0.099609375).astype(jnp.bfloat16)
    gossip_round = jax.random.randint(key_of[5], (1,), 0, ROUNDS).astype(jnp.int32)
    step_count = jax.random.randint(key_of[6], (1,), 1, 9).astype(jnp.int32)
    return {"activations": activations, "out_grads": out_grads, "params": params, "first_moment": first_moment, "second_moment": second_moment, "gossip_round": gossip_round, "step_count": step_count}


def replica_update(items, bias_one, bias_two):
    act_block, out_block, weight, moment_a, moment_b = items
    gradient = jnp.dot(act_block.T, out_block, preferred_element_type=jnp.float32)
    moment_one = 0.9 * moment_a.astype(jnp.float32) + 0.1 * gradient
    moment_two = 0.999 * moment_b.astype(jnp.float32) + 0.001 * gradient * gradient
    update = moment_one / bias_one / (jnp.sqrt(moment_two / bias_two) + 1e-08)
    stepped = (weight.astype(jnp.float32) * (1.0 - 0.02 * 0.1) - 0.02 * update).astype(jnp.bfloat16)
    return (stepped, moment_one.astype(jnp.bfloat16))

def reference(activations, out_grads, params, first_moment, second_moment, gossip_round, step_count):
    count_float = step_count[0].astype(jnp.float32)
    bias_one = 1.0 - jnp.power(jnp.float32(0.9), count_float)
    bias_two = 1.0 - jnp.power(jnp.float32(0.999), count_float)
    stepped, new_moment = lax.map(lambda items: replica_update(items, bias_one, bias_two), (activations, out_grads, params, first_moment, second_moment))
    offset = jnp.power(jnp.int32(2), gossip_round[0].astype(jnp.int32))
    received = jnp.roll(stepped, offset, axis=0)
    averaged = (0.5 * (stepped.astype(jnp.float32) + received.astype(jnp.float32))).astype(jnp.bfloat16)
    return (averaged, new_moment)
```

```python
import functools
import math

import jax
import jax.numpy as jnp
from jax import lax
from jax.experimental import pallas as pl
from jax.experimental.pallas import tpu as pltpu
from jax.sharding import PartitionSpec as P

ROUNDS = 3
LANES = 128
WIDTHS = (5, 5, 4)
BF16 = jnp.bfloat16
F32 = jnp.float32
VMEM_LIMIT = 48 * 1024 * 1024

UNIT = 2.0**-12
CODE = 32767.0 / math.log1p(2.0**11 / UNIT)


def encode(g):
    level = jnp.log(1.0 + jnp.abs(g) * (1.0 / UNIT)) * CODE
    level = jnp.minimum(jnp.floor(level + 0.5), 32767.0)
    return jnp.where(g < 0.0, -level, level).astype(jnp.int32).astype(jnp.int16)


def decode(q):
    level = q.astype(jnp.int32).astype(F32)
    size = (jnp.exp(jnp.abs(level) * (1.0 / CODE)) - 1.0) * UNIT
    return jnp.where(level < 0.0, -size, size)


def chunks(total):
    out, at = [], 0
    for i, tiles in enumerate(WIDTHS):
        width = tiles * LANES
        if i == len(WIDTHS) - 1:
            at = total - 4 * width
        out.append((at, width))
        at += 4 * width
    return out


def params_of(**kw):
    return pltpu.CompilerParams(vmem_limit_bytes=VMEM_LIMIT, **kw)


SMEM = pl.BlockSpec(memory_space=pltpu.SMEM)
VMEM = pl.BlockSpec(memory_space=pltpu.VMEM)
HBM = pl.BlockSpec(memory_space=pl.ANY)


def cols(start, width):
    return pl.ds(pl.multiple_of(start, LANES), width)


def first_kernel(plan, place, act, dy, a0, a1, a2, a3, csend):
    y, c = place[0], place[2]
    rows = a0.shape[0]
    for r, out in enumerate((a0, a1, a2, a3)):
        quarter = lax.rem(y + r, 4)
        out[...] = act[:, cols(quarter * rows, rows)].T
    at = 0
    for start, width in plan:
        for x in range(2):
            csend[:, at : at + width] = dy[:, cols(start + (x * 2 + 1 - c) * width, width)]
            at += width


def split_kernel(plan, place, dy, crecv, *outs):
    x, c = place[1], place[2]
    tokens = dy.shape[0]
    at = 0
    for j, (start, width) in enumerate(plan):
        for far in range(2):
            side = x if far == 0 else 1 - x
            out = outs[2 * j + far]
            out[:tokens, :] = dy[:, cols(start + (side * 2 + c) * width, width)]
            out[tokens:, :] = crecv[:, cols(at + side * width, width)]
        at += 2 * width


def matmul_kernel(place, b0, bc, bx, bxc, *rest):
    pieces, outs = rest[:8], rest[8:12]
    lhs, rhs, acc, sems = rest[12:]
    x, c = place[1], place[2]
    quarter, tokens = b0.shape[1], b0.shape[2]
    copies = []
    for i in range(4):
        for k, b in enumerate((b0, bc, bx, bxc)):
            copies.append((b.at[i], lhs.at[:, (i * 4 + k) * tokens : (i * 4 + k + 1) * tokens]))
        for k in range(2):
            p = pieces[2 * i + k]
            depth = 2 * tokens
            copies.append((p, rhs.at[(2 * i + k) * depth : (2 * i + k + 1) * depth]))
    copies = [pltpu.make_async_copy(s, d, sems.at[n]) for n, (s, d) in enumerate(copies)]
    for copy in copies:
        copy.start()
    for copy in copies:
        copy.wait()
    acc[...] = jnp.dot(lhs[...], rhs[...], preferred_element_type=F32)
    rows = quarter // 4
    for k, out in enumerate(outs):
        dx, dc = k // 2, k % 2
        xx = x if dx == 0 else 1 - x
        cc = c if dc == 0 else 1 - c
        block = pl.ds(pl.multiple_of((xx * 2 + cc) * rows, 16), rows)
        out[...] = encode(acc[block, :])


def adam_kernel(start, width, n_prev, place, bias, *rest):
    g = rest[:4]
    params, first, second = rest[4:7]
    rest = rest[7 + n_prev :]
    stepped, moment, pv, fv, sv, mv, sems = rest
    x, c = place[1], place[2]
    rows = stepped.shape[0]
    window = pl.ds(start, 4 * width)
    loads = [
        pltpu.make_async_copy(src.at[:, window], dst, sems.at[n])
        for n, (src, dst) in enumerate(((params, pv), (first, fv), (second, sv)))
    ]
    for copy in loads:
        copy.start()
    for copy in loads:
        copy.wait()
    inv_one, inv_two = bias[0], bias[1]
    step = 32
    for k in range(4):
        dx, dc = k // 2, k % 2
        xx = x if dx == 0 else 1 - x
        cc = c if dc == 0 else 1 - c
        where = cols((xx * 2 + cc) * width, width)

        def body(i, _, k=k, where=where):
            r = pl.ds(pl.multiple_of(i * step, step), step)
            grad = decode(g[k][r, :])
            one = 0.9 * fv[r, where].astype(F32) + 0.1 * grad
            two = 0.999 * sv[r, where].astype(F32) + 0.001 * grad * grad
            update = (one * inv_one) / (jnp.sqrt(two * inv_two) + 1e-08)
            new = pv[r, where].astype(F32) * (1.0 - 0.02 * 0.1) - 0.02 * update
            stepped[r, where] = new.astype(BF16)
            mv[r, where] = one.astype(BF16)
            return 0

        lax.fori_loop(0, rows // step, body, 0)
    out = pltpu.make_async_copy(mv, moment.at[:, window], sems.at[3])
    out.start()
    out.wait()


def average_kernel(start, n_prev, own, other, *rest):
    averaged, buf, sem = rest[n_prev:]
    buf[...] = (0.5 * (own[...].astype(F32) + other[...].astype(F32))).astype(BF16)
    out = pltpu.make_async_copy(buf, averaged.at[:, pl.ds(start, buf.shape[1])], sem)
    out.start()
    out.wait()


def moved(block, dy=0, dx=0, dc=0):
    route = []
    for i in range(16):
        y, x, c = i // 4, i // 2 % 2, i % 2
        route.append((i, ((y + dy) % 4 * 2 + (x + dx) % 2) * 2 + (c + dc) % 2))
    return lax.ppermute(block, "shard", route)


def gossip(block, offset):
    return lax.ppermute(block, "gossip", [(i, (i + offset) % 16) for i in range(16)])


def body(offset, act, dy, params, first, second, place, bias):
    tokens, depth = act.shape
    total = dy.shape[1]
    rows = params.shape[0]
    quarter = depth // 4
    plan = chunks(total)
    half = sum(2 * w for _, w in plan)
    shape = jax.ShapeDtypeStruct
    with jax.named_scope("arrange"):
        a0, a1, a2, a3, csend = pl.pallas_call(
            functools.partial(first_kernel, plan),
            out_shape=[shape((quarter, tokens), BF16)] * 4 + [shape((tokens, half), BF16)],
            in_specs=[SMEM, VMEM, VMEM],
            out_specs=[VMEM] * 5,
            compiler_params=params_of(),
        )(place, act, dy)
        crecv = moved(csend, dc=1)
        split = pl.pallas_call(
            functools.partial(split_kernel, plan),
            out_shape=[shape((2 * tokens, w), BF16) for _, w in plan for _ in range(2)],
            in_specs=[SMEM, VMEM, VMEM],
            out_specs=[VMEM] * (2 * len(plan)),
            compiler_params=params_of(),
        )(place, dy, crecv)
    with jax.named_scope("activations"):
        b0 = jnp.stack([a0, moved(a1, dy=1), moved(a3, dy=3), moved(a2, dy=2)])
        bc = moved(b0, dc=1)
        bx = moved(b0, dx=1)
        bxc = moved(bx, dc=1)

    moment = averaged = None
    for j, (start, width) in enumerate(plan):
        with jax.named_scope("gather"):
            own = split[2 * j]
            far = moved(split[2 * j + 1], dx=1)
            own_l, own_r = moved(own, dy=1), moved(own, dy=3)
            far_l, far_r = moved(far, dy=1), moved(far, dy=3)
            own_o, far_o = moved(own_l, dy=1), moved(far_r, dy=3)
        pieces = (own, far, own_l, far_l, own_r, far_r, own_o, far_o)
        with jax.named_scope("gradient"):
            codes = pl.pallas_call(
                matmul_kernel,
                out_shape=[shape((rows, width), jnp.int16)] * 4,
                in_specs=[SMEM] + [HBM] * 12,
                out_specs=[VMEM] * 4,
                scratch_shapes=[
                    pltpu.VMEM((quarter, 16 * tokens), BF16),
                    pltpu.VMEM((16 * tokens, width), BF16),
                    pltpu.VMEM((quarter, width), F32),
                    pltpu.SemaphoreType.DMA((24,)),
                ],
                compiler_params=params_of(),
                cost_estimate=pl.CostEstimate(
                    flops=2 * quarter * width * 16 * tokens,
                    bytes_accessed=2 * 16 * tokens * (quarter + width),
                    transcendentals=quarter * width,
                ),
            )(place, b0, bc, bx, bxc, *pieces)
            grads = [
                codes[0],
                moved(codes[1], dc=1),
                moved(codes[2], dx=1),
                moved(codes[3], dx=1, dc=1),
            ]
        with jax.named_scope("adam"):
            previous = [] if moment is None else [moment]
            stepped, moment = pl.pallas_call(
                functools.partial(adam_kernel, start, width, len(previous)),
                out_shape=[shape((rows, 4 * width), BF16), shape((rows, total), BF16)],
                in_specs=[SMEM, SMEM] + [VMEM] * 4 + [HBM] * (3 + len(previous)),
                out_specs=[VMEM, HBM],
                scratch_shapes=[pltpu.VMEM((rows, 4 * width), BF16)] * 4
                + [pltpu.SemaphoreType.DMA((4,))],
                input_output_aliases={9: 1} if previous else {},
                compiler_params=params_of(),
                cost_estimate=pl.CostEstimate(
                    flops=100 * rows * width,
                    bytes_accessed=48 * rows * width,
                    transcendentals=12 * rows * width,
                ),
            )(place, bias, *grads, params, first, second, *previous)
        with jax.named_scope("average"):
            received = gossip(stepped, offset)
            previous = [] if averaged is None else [averaged]
            averaged = pl.pallas_call(
                functools.partial(average_kernel, start, len(previous)),
                out_shape=shape((rows, total), BF16),
                in_specs=[VMEM, VMEM] + [HBM] * len(previous),
                out_specs=HBM,
                scratch_shapes=[pltpu.VMEM((rows, 4 * width), BF16), pltpu.SemaphoreType.DMA],
                input_output_aliases={2: 0} if previous else {},
                compiler_params=params_of(),
                cost_estimate=pl.CostEstimate(
                    flops=12 * rows * width, bytes_accessed=24 * rows * width, transcendentals=0
                ),
            )(stepped, received, *previous)
    return averaged, moment


def per_device(
    activations, out_grads, params, first_moment, second_moment, gossip_round, step_count
):
    index = lax.axis_index("shard")
    place = jnp.stack([index // 4, index // 2 % 2, index % 2]).astype(jnp.int32)
    count_float = step_count[0].astype(F32)
    bias_one = 1.0 - jnp.power(F32(0.9), count_float)
    bias_two = 1.0 - jnp.power(F32(0.999), count_float)
    bias = jnp.stack([1.0 / bias_one, 1.0 / bias_two])
    averaged, moment = lax.switch(
        gossip_round[0],
        [functools.partial(body, 2**k) for k in range(ROUNDS)],
        activations[0],
        out_grads[0],
        params[0],
        first_moment[0],
        second_moment[0],
        place,
        bias,
    )
    return averaged[None], moment[None]


def solution(mesh):
    spec = P("gossip", "shard", None)
    return jax.shard_map(
        per_device,
        mesh=mesh,
        in_specs=(spec,) * 5 + (P(), P()),
        out_specs=(spec, spec),
        check_vma=False,
    )
```

```python
import functools
import math

import jax
import jax.numpy as jnp
from jax import lax
from jax.experimental import pallas as pl
from jax.experimental.pallas import tpu as pltpu
from jax.sharding import PartitionSpec as P

ROUNDS = 3
LANES = 128
BRANCHED = True
WIDTHS = (4, 6, 4)
BF16 = jnp.bfloat16
F32 = jnp.float32
LIGHT = pl.CostEstimate(flops=1, bytes_accessed=1, transcendentals=0)
VMEM_LIMIT = 48 * 1024 * 1024

UNIT = 2.0**-12
CODE = 32767.0 / math.log1p(2.0**11 / UNIT)


def encode(g):
    level = jnp.log(1.0 + jnp.abs(g) * (1.0 / UNIT)) * CODE
    level = jnp.minimum(jnp.floor(level + 0.5), 32767.0)
    return jnp.where(g < 0.0, -level, level).astype(jnp.int32).astype(jnp.int16)


def decode(q):
    level = q.astype(jnp.int32).astype(F32)
    size = (jnp.exp(jnp.abs(level) * (1.0 / CODE)) - 1.0) * UNIT
    return jnp.where(level < 0.0, -size, size)


def chunks(total):
    out, at = [], 0
    for i, tiles in enumerate(WIDTHS):
        width = tiles * LANES
        if i == len(WIDTHS) - 1:
            at = total - 4 * width
        out.append((at, width))
        at += 4 * width
    return out


def params_of(**kw):
    return pltpu.CompilerParams(vmem_limit_bytes=VMEM_LIMIT, **kw)


SMEM = pl.BlockSpec(memory_space=pltpu.SMEM)
VMEM = pl.BlockSpec(memory_space=pltpu.VMEM)
HBM = pl.BlockSpec(memory_space=pl.ANY)


def cols(start, width):
    return pl.ds(pl.multiple_of(start, LANES), width)


def first_kernel(plan, place, act, dy, a0, a1, a2, a3, csend):
    y, c = place[0], place[2]
    rows = a0.shape[0]
    for r, out in enumerate((a0, a1, a2, a3)):
        quarter = lax.rem(y + r, 4)
        out[...] = act[:, cols(quarter * rows, rows)].T
    at = 0
    for start, width in plan:
        for x in range(2):
            csend[:, at : at + width] = dy[:, cols(start + (x * 2 + 1 - c) * width, width)]
            at += width


def split_kernel(start, width, at, place, dy, crecv, *rest):
    near, far = rest[-2:]
    x, c = place[1], place[2]
    tokens = dy.shape[0]
    for side, out in ((x, near), (1 - x, far)):
        out[:tokens, :] = dy[:, cols(start + (side * 2 + c) * width, width)]
        out[tokens:, :] = crecv[:, cols(at + side * width, width)]


def stack_kernel(p0, p1, p2, p3, *rest):
    out, sems = rest[-2:]
    copies = [
        pltpu.make_async_copy(p, out.at[n], sems.at[n]) for n, p in enumerate((p0, p1, p2, p3))
    ]
    for copy in copies:
        copy.start()
    for copy in copies:
        copy.wait()


def matmul_kernel(n_order, place, b0, bc, bx, bxc, *rest):
    pieces, rest = rest[:8], rest[8 + n_order :]
    outs = rest[:4]
    lhs, rhs, acc, sems = rest[4:]
    x, c = place[1], place[2]
    quarter, tokens = b0.shape[1], b0.shape[2]
    copies = []
    for i in range(4):
        for k, b in enumerate((b0, bc, bx, bxc)):
            copies.append((b.at[i], lhs.at[:, (i * 4 + k) * tokens : (i * 4 + k + 1) * tokens]))
        for k in range(2):
            p = pieces[2 * i + k]
            depth = 2 * tokens
            copies.append((p, rhs.at[(2 * i + k) * depth : (2 * i + k + 1) * depth]))
    copies = [pltpu.make_async_copy(s, d, sems.at[n]) for n, (s, d) in enumerate(copies)]
    for copy in copies:
        copy.start()
    for copy in copies:
        copy.wait()
    width = rhs.shape[1]
    part = 256 if width % 256 == 0 else LANES

    def columns(n, _):
        where = cols(n * part, part)
        acc[:, where] = jnp.dot(lhs[...], rhs[:, where], preferred_element_type=F32)
        return 0

    lax.fori_loop(0, width // part, columns, 0)
    rows = quarter // 4
    step = 16
    for k, out in enumerate(outs):
        dx, dc = k // 2, k % 2
        xx = x if dx == 0 else 1 - x
        cc = c if dc == 0 else 1 - c
        base = (xx * 2 + cc) * rows

        def some(i, _, base=base, out=out):
            r = pl.ds(pl.multiple_of(i * step, step), step)
            out[r, :] = encode(acc[pl.ds(pl.multiple_of(base + i * step, step), step), :])
            return 0

        lax.fori_loop(0, rows // step, some, 0)


def adam_kernel(start, width, n_prev, place, bias, *rest):
    g = rest[:4]
    params, first, second = rest[4:7]
    rest = rest[7 + n_prev :]
    stepped, moment, pv, fv, sv, mv, sems = rest
    x, c = place[1], place[2]
    rows = stepped.shape[0]
    window = pl.ds(start, 4 * width)
    loads = [
        pltpu.make_async_copy(src.at[:, window], dst, sems.at[n])
        for n, (src, dst) in enumerate(((params, pv), (first, fv), (second, sv)))
    ]
    for copy in loads:
        copy.start()
    for copy in loads:
        copy.wait()
    inv_one, inv_two = bias[0], bias[1]
    step = 16
    for k in range(4):
        dx, dc = k // 2, k % 2
        xx = x if dx == 0 else 1 - x
        cc = c if dc == 0 else 1 - c
        where = cols((xx * 2 + cc) * width, width)

        def body(i, _, k=k, where=where):
            r = pl.ds(pl.multiple_of(i * step, step), step)
            grad = decode(g[k][r, :])
            one = 0.9 * fv[r, where].astype(F32) + 0.1 * grad
            two = 0.999 * sv[r, where].astype(F32) + 0.001 * grad * grad
            update = (one * inv_one) / (jnp.sqrt(two * inv_two) + 1e-08)
            new = pv[r, where].astype(F32) * (1.0 - 0.02 * 0.1) - 0.02 * update
            stepped[r, where] = new.astype(BF16)
            mv[r, where] = one.astype(BF16)
            return 0

        lax.fori_loop(0, rows // step, body, 0)
    out = pltpu.make_async_copy(mv, moment.at[:, window], sems.at[3])
    out.start()
    out.wait()


def average_kernel(start, n_prev, own, other, *rest):
    averaged, buf, sem = rest[n_prev:]
    buf[...] = (0.5 * (own[...].astype(F32) + other[...].astype(F32))).astype(BF16)
    out = pltpu.make_async_copy(buf, averaged.at[:, pl.ds(start, buf.shape[1])], sem)
    out.start()
    out.wait()


def moved(block, dy=0, dx=0, dc=0):
    route = []
    for i in range(16):
        y, x, c = i // 4, i // 2 % 2, i % 2
        route.append((i, ((y + dy) % 4 * 2 + (x + dx) % 2) * 2 + (c + dc) % 2))
    return lax.ppermute(block, "shard", route)


def gossip(block, offset, which):
    if offset is None:
        shifts = [functools.partial(gossip, offset=2**k, which=which) for k in range(ROUNDS)]
        return lax.switch(which, shifts, block)
    return lax.ppermute(block, "gossip", [(i, (i + offset) % 16) for i in range(16)])


def body(offset, act, dy, params, first, second, place, bias, which):
    tokens, depth = act.shape
    total = dy.shape[1]
    rows = params.shape[0]
    quarter = depth // 4
    plan = chunks(total)
    half = sum(2 * w for _, w in plan)
    shape = jax.ShapeDtypeStruct
    with jax.named_scope("arrange"):
        a0, a1, a2, a3, csend = pl.pallas_call(
            functools.partial(first_kernel, plan),
            out_shape=[shape((quarter, tokens), BF16)] * 4 + [shape((tokens, half), BF16)],
            in_specs=[SMEM, VMEM, VMEM],
            out_specs=[VMEM] * 5,
            compiler_params=params_of(),
        cost_estimate=LIGHT,
        )(place, act, dy)
        crecv = moved(csend, dc=1)

    def split(j, at, order):
        start, width = plan[j]
        with jax.named_scope("arrange"):
            return pl.pallas_call(
                functools.partial(split_kernel, start, width, at),
                out_shape=[shape((2 * tokens, width), BF16)] * 2,
                in_specs=[SMEM, VMEM, VMEM] + [HBM] * len(order),
                out_specs=[VMEM] * 2,
                compiler_params=params_of(),
        cost_estimate=LIGHT,
            )(place, dy, crecv, *order)

    splits = [sum(2 * w for _, w in plan[:j]) for j in range(len(plan))]
    near, far_out = [None] * len(plan), [None] * len(plan)
    far = [None] * len(plan)

    def send(j, order):
        near[j], far_out[j] = split(j, splits[j], order)
        with jax.named_scope("gather"):
            far[j] = moved(far_out[j], dx=1)

    ring = {}

    def circulate(j):
        with jax.named_scope("gather"):
            own_l, own_r = moved(near[j], dy=1), moved(near[j], dy=3)
            far_r, far_l = moved(far[j], dy=3), moved(far[j], dy=1)
            own_o, far_o = moved(own_l, dy=1), moved(far_r, dy=3)
        ring[j] = (near[j], far[j], own_l, far_l, own_r, far_r, own_o, far_o)

    send(0, [])
    send(1, [far[0]])
    circulate(0)
    circulate(1)
    with jax.named_scope("activations"):
        order = [far[0]]
        b0 = pl.pallas_call(
            stack_kernel,
            out_shape=shape((4, quarter, tokens), BF16),
            in_specs=[HBM] * (4 + len(order)),
            out_specs=HBM,
            scratch_shapes=[pltpu.SemaphoreType.DMA((4,))],
            compiler_params=params_of(),
            cost_estimate=LIGHT,
        )(a0, moved(a1, dy=1), moved(a3, dy=3), moved(a2, dy=2), *order)
        bc = moved(b0, dc=1)
        bx = moved(b0, dx=1)
        bxc = moved(bx, dc=1)
    if len(plan) > 2:
        send(2, [bx, ring[1][2]])
        circulate(2)

    moment = averaged = None
    history = []
    for j, (start, width) in enumerate(plan):
        if j > 2:
            send(j, [history[j - 3][0]])
            circulate(j)
        pieces = ring[j]
        order = [far[2]] if j == 0 and len(plan) > 2 else []
        if j > 0:
            order.append(history[j - 1][1])
        if j > 1:
            order.append(history[j - 2][2])
        with jax.named_scope("gradient"):
            codes = pl.pallas_call(
                functools.partial(matmul_kernel, len(order)),
                out_shape=[shape((rows, width), jnp.int16)] * 4,
                in_specs=[SMEM] + [HBM] * (12 + len(order)),
                out_specs=[VMEM] * 4,
                scratch_shapes=[
                    pltpu.VMEM((quarter, 16 * tokens), BF16),
                    pltpu.VMEM((16 * tokens, width), BF16),
                    pltpu.VMEM((quarter, width), F32),
                    pltpu.SemaphoreType.DMA((24,)),
                ],
                compiler_params=params_of(),
        cost_estimate=LIGHT,
            )(place, b0, bc, bx, bxc, *pieces, *order)
            grads = [
                codes[0],
                moved(codes[1], dc=1),
                moved(codes[2], dx=1),
                moved(codes[3], dx=1, dc=1),
            ]
        with jax.named_scope("adam"):
            previous = [] if moment is None else [moment]
            stepped, moment = pl.pallas_call(
                functools.partial(adam_kernel, start, width, len(previous)),
                out_shape=[shape((rows, 4 * width), BF16), shape((rows, total), BF16)],
                in_specs=[SMEM, SMEM] + [VMEM] * 4 + [HBM] * (3 + len(previous)),
                out_specs=[VMEM, HBM],
                scratch_shapes=[pltpu.VMEM((rows, 4 * width), BF16)] * 4
                + [pltpu.SemaphoreType.DMA((4,))],
                input_output_aliases={9: 1} if previous else {},
                compiler_params=params_of(),
        cost_estimate=LIGHT,
            )(place, bias, *grads, params, first, second, *previous)
        with jax.named_scope("average"):
            received = gossip(stepped, offset, which)
            history.append((codes[0], grads[2], received))
            previous = [] if averaged is None else [averaged]
            averaged = pl.pallas_call(
                functools.partial(average_kernel, start, len(previous)),
                out_shape=shape((rows, total), BF16),
                in_specs=[VMEM, VMEM] + [HBM] * len(previous),
                out_specs=HBM,
                scratch_shapes=[pltpu.VMEM((rows, 4 * width), BF16), pltpu.SemaphoreType.DMA],
                input_output_aliases={2: 0} if previous else {},
                compiler_params=params_of(),
        cost_estimate=LIGHT,
            )(stepped, received, *previous)
    return averaged, moment


def per_device(
    activations, out_grads, params, first_moment, second_moment, gossip_round, step_count
):
    index = lax.axis_index("shard")
    place = jnp.stack([index // 4, index // 2 % 2, index % 2]).astype(jnp.int32)
    count_float = step_count[0].astype(F32)
    bias_one = 1.0 - jnp.power(F32(0.9), count_float)
    bias_two = 1.0 - jnp.power(F32(0.999), count_float)
    bias = jnp.stack([1.0 / bias_one, 1.0 / bias_two])
    operands = (
        activations[0],
        out_grads[0],
        params[0],
        first_moment[0],
        second_moment[0],
        place,
        bias,
        gossip_round[0],
    )
    if BRANCHED:
        averaged, moment = lax.switch(
            ROUNDS - 1 - gossip_round[0],
            [functools.partial(body, 2**k) for k in reversed(range(ROUNDS))],
            *operands,
        )
    else:
        averaged, moment = body(None, *operands)
    return averaged[None], moment[None]


def solution(mesh):
    spec = P("gossip", "shard", None)
    return jax.shard_map(
        per_device,
        mesh=mesh,
        in_specs=(spec,) * 5 + (P(), P()),
        out_specs=(spec, spec),
        check_vma=False,
    )
```

```python
import functools
import math

import jax
import jax.numpy as jnp
from jax import lax
from jax.experimental import pallas as pl
from jax.experimental.pallas import tpu as pltpu
from jax.sharding import PartitionSpec as P

ROUNDS = 3
LANES = 128
BRANCHED = True
WIDTHS = (4, 6, 4)
BF16 = jnp.bfloat16
F32 = jnp.float32
LIGHT = pl.CostEstimate(flops=1, bytes_accessed=1, transcendentals=0)
VMEM_LIMIT = 48 * 1024 * 1024

UNIT = 2.0**-12
CODE = 32767.0 / math.log1p(2.0**11 / UNIT)


def encode(g):
    level = jnp.log(1.0 + jnp.abs(g) * (1.0 / UNIT)) * CODE
    level = jnp.minimum(jnp.floor(level + 0.5), 32767.0)
    return jnp.where(g < 0.0, -level, level).astype(jnp.int32).astype(jnp.int16)


def decode(q):
    level = q.astype(jnp.int32).astype(F32)
    size = (jnp.exp(jnp.abs(level) * (1.0 / CODE)) - 1.0) * UNIT
    return jnp.where(level < 0.0, -size, size)


def chunks(total):
    out, at = [], 0
    for i, tiles in enumerate(WIDTHS):
        width = tiles * LANES
        if i == len(WIDTHS) - 1:
            at = total - 4 * width
        out.append((at, width))
        at += 4 * width
    return out


def params_of(**kw):
    return pltpu.CompilerParams(vmem_limit_bytes=VMEM_LIMIT, **kw)


SMEM = pl.BlockSpec(memory_space=pltpu.SMEM)
VMEM = pl.BlockSpec(memory_space=pltpu.VMEM)
HBM = pl.BlockSpec(memory_space=pl.ANY)


def cols(start, width):
    return pl.ds(pl.multiple_of(start, LANES), width)


def first_kernel(plan, place, act, dy, a0, a1, a2, a3, csend):
    y, c = place[0], place[2]
    rows = a0.shape[0]
    for r, out in enumerate((a0, a1, a2, a3)):
        quarter = lax.rem(y + r, 4)
        out[...] = act[:, cols(quarter * rows, rows)].T
    at = 0
    for start, width in plan:
        for x in range(2):
            csend[:, at : at + width] = dy[:, cols(start + (x * 2 + 1 - c) * width, width)]
            at += width


def split_kernel(start, width, at, place, dy, crecv, *rest):
    near, far = rest[-2:]
    x, c = place[1], place[2]
    tokens = dy.shape[0]
    for side, out in ((x, near), (1 - x, far)):
        out[:tokens, :] = dy[:, cols(start + (side * 2 + c) * width, width)]
        out[tokens:, :] = crecv[:, cols(at + side * width, width)]


def stack_kernel(p0, p1, p2, p3, *rest):
    out, sems = rest[-2:]
    copies = [
        pltpu.make_async_copy(p, out.at[n], sems.at[n]) for n, p in enumerate((p0, p1, p2, p3))
    ]
    for copy in copies:
        copy.start()
    for copy in copies:
        copy.wait()


def matmul_kernel(n_order, place, b0, bc, bx, bxc, *rest):
    pieces, rest = rest[:8], rest[8 + n_order :]
    outs = rest[:4]
    lhs, rhs, acc, sems = rest[4:]
    x, c = place[1], place[2]
    quarter, tokens = b0.shape[1], b0.shape[2]
    copies = []
    for i in range(4):
        for k, b in enumerate((b0, bc, bx, bxc)):
            copies.append((b.at[i], lhs.at[:, (i * 4 + k) * tokens : (i * 4 + k + 1) * tokens]))
        for k in range(2):
            p = pieces[2 * i + k]
            depth = 2 * tokens
            copies.append((p, rhs.at[(2 * i + k) * depth : (2 * i + k + 1) * depth]))
    copies = [pltpu.make_async_copy(s, d, sems.at[n]) for n, (s, d) in enumerate(copies)]
    for copy in copies:
        copy.start()
    for copy in copies:
        copy.wait()
    width = rhs.shape[1]
    part = 256 if width % 256 == 0 else LANES

    def columns(n, _):
        where = cols(n * part, part)
        acc[:, where] = jnp.dot(lhs[...], rhs[:, where], preferred_element_type=F32)
        return 0

    lax.fori_loop(0, width // part, columns, 0)
    rows = quarter // 4
    step = 16
    for k, out in enumerate(outs):
        dx, dc = k // 2, k % 2
        xx = x if dx == 0 else 1 - x
        cc = c if dc == 0 else 1 - c
        base = (xx * 2 + cc) * rows

        def some(i, _, base=base, out=out):
            r = pl.ds(pl.multiple_of(i * step, step), step)
            out[r, :] = encode(acc[pl.ds(pl.multiple_of(base + i * step, step), step), :])
            return 0

        lax.fori_loop(0, rows // step, some, 0)


def adam_kernel(start, width, n_prev, place, bias, *rest):
    g = rest[:4]
    params, first, second = rest[4:7]
    rest = rest[7 + n_prev :]
    stepped, moment, pv, fv, sv, mv, sems = rest
    x, c = place[1], place[2]
    rows = stepped.shape[0]
    window = pl.ds(start, 4 * width)
    loads = [
        pltpu.make_async_copy(src.at[:, window], dst, sems.at[n])
        for n, (src, dst) in enumerate(((params, pv), (first, fv), (second, sv)))
    ]
    for copy in loads:
        copy.start()
    for copy in loads:
        copy.wait()
    inv_one, inv_two = bias[0], bias[1]
    step = 16
    for k in range(4):
        dx, dc = k // 2, k % 2
        xx = x if dx == 0 else 1 - x
        cc = c if dc == 0 else 1 - c
        where = cols((xx * 2 + cc) * width, width)

        def body(i, _, k=k, where=where):
            r = pl.ds(pl.multiple_of(i * step, step), step)
            grad = decode(g[k][r, :])
            one = 0.9 * fv[r, where].astype(F32) + 0.1 * grad
            two = 0.999 * sv[r, where].astype(F32) + 0.001 * grad * grad
            update = (one * inv_one) / (jnp.sqrt(two * inv_two) + 1e-08)
            new = pv[r, where].astype(F32) * (1.0 - 0.02 * 0.1) - 0.02 * update
            stepped[r, where] = new.astype(BF16)
            mv[r, where] = one.astype(BF16)
            return 0

        lax.fori_loop(0, rows // step, body, 0)
    out = pltpu.make_async_copy(mv, moment.at[:, window], sems.at[3])
    out.start()
    out.wait()


def average_kernel(start, n_prev, own, other, *rest):
    averaged, buf, sem = rest[n_prev:]
    buf[...] = (0.5 * (own[...].astype(F32) + other[...].astype(F32))).astype(BF16)
    out = pltpu.make_async_copy(buf, averaged.at[:, pl.ds(start, buf.shape[1])], sem)
    out.start()
    out.wait()


def moved(block, dy=0, dx=0, dc=0):
    route = []
    for i in range(16):
        y, x, c = i // 4, i // 2 % 2, i % 2
        route.append((i, ((y + dy) % 4 * 2 + (x + dx) % 2) * 2 + (c + dc) % 2))
    return lax.ppermute(block, "shard", route)


def gossip(block, offset, which):
    if offset is None:
        shifts = [functools.partial(gossip, offset=2**k, which=which) for k in range(ROUNDS)]
        return lax.switch(which, shifts, block)
    return lax.ppermute(block, "gossip", [(i, (i + offset) % 16) for i in range(16)])


def body(offset, act, dy, params, first, second, place, bias, which):
    tokens, depth = act.shape
    total = dy.shape[1]
    rows = params.shape[0]
    quarter = depth // 4
    plan = chunks(total)
    half = sum(2 * w for _, w in plan)
    shape = jax.ShapeDtypeStruct
    with jax.named_scope("arrange"):
        a0, a1, a2, a3, csend = pl.pallas_call(
            functools.partial(first_kernel, plan),
            out_shape=[shape((quarter, tokens), BF16)] * 4 + [shape((tokens, half), BF16)],
            in_specs=[SMEM, VMEM, VMEM],
            out_specs=[VMEM] * 5,
            compiler_params=params_of(),
        cost_estimate=LIGHT,
        )(place, act, dy)
        crecv = moved(csend, dc=1)

    def split(j, at, order):
        start, width = plan[j]
        with jax.named_scope("arrange"):
            return pl.pallas_call(
                functools.partial(split_kernel, start, width, at),
                out_shape=[shape((2 * tokens, width), BF16)] * 2,
                in_specs=[SMEM, VMEM, VMEM] + [HBM] * len(order),
                out_specs=[VMEM] * 2,
                compiler_params=params_of(),
        cost_estimate=LIGHT,
            )(place, dy, crecv, *order)

    splits = [sum(2 * w for _, w in plan[:j]) for j in range(len(plan))]
    near, far_out = [None] * len(plan), [None] * len(plan)
    far = [None] * len(plan)

    def send(j, order):
        near[j], far_out[j] = split(j, splits[j], order)
        with jax.named_scope("gather"):
            far[j] = moved(far_out[j], dx=1)

    ring = {}

    def circulate(j):
        with jax.named_scope("gather"):
            own_l, own_r = moved(near[j], dy=1), moved(near[j], dy=3)
            far_r, far_l = moved(far[j], dy=3), moved(far[j], dy=1)
            own_o, far_o = moved(own_l, dy=1), moved(far_r, dy=3)
        ring[j] = (near[j], far[j], own_l, far_l, own_r, far_r, own_o, far_o)

    send(0, [])
    send(1, [far[0]])
    circulate(0)
    circulate(1)
    with jax.named_scope("activations"):
        order = [far[0]]
        b0 = pl.pallas_call(
            stack_kernel,
            out_shape=shape((4, quarter, tokens), BF16),
            in_specs=[HBM] * (4 + len(order)),
            out_specs=HBM,
            scratch_shapes=[pltpu.SemaphoreType.DMA((4,))],
            compiler_params=params_of(),
            cost_estimate=LIGHT,
        )(a0, moved(a1, dy=1), moved(a3, dy=3), moved(a2, dy=2), *order)
        bc = moved(b0, dc=1)
        bx = moved(b0, dx=1)
        bxc = moved(bx, dc=1)
    if len(plan) > 2:
        send(2, [bx, ring[1][2]])
        circulate(2)

    moment = averaged = None
    history = []
    for j, (start, width) in enumerate(plan):
        if j > 2:
            send(j, [history[j - 3][0]])
            circulate(j)
        pieces = ring[j]
        order = [far[2]] if j == 0 and len(plan) > 2 else []
        if j > 0:
            order.append(history[j - 1][1])
        if j > 1:
            order.append(history[j - 2][2])
        with jax.named_scope("gradient"):
            codes = pl.pallas_call(
                functools.partial(matmul_kernel, len(order)),
                out_shape=[shape((rows, width), jnp.int16)] * 4,
                in_specs=[SMEM] + [HBM] * (12 + len(order)),
                out_specs=[VMEM] * 4,
                scratch_shapes=[
                    pltpu.VMEM((quarter, 16 * tokens), BF16),
                    pltpu.VMEM((16 * tokens, width), BF16),
                    pltpu.VMEM((quarter, width), F32),
                    pltpu.SemaphoreType.DMA((24,)),
                ],
                compiler_params=params_of(),
        cost_estimate=LIGHT,
            )(place, b0, bc, bx, bxc, *pieces, *order)
            grads = [
                codes[0],
                moved(codes[1], dc=1),
                moved(codes[2], dx=1),
                moved(codes[3], dx=1, dc=1),
            ]
        with jax.named_scope("adam"):
            previous = [] if moment is None else [moment]
            stepped, moment = pl.pallas_call(
                functools.partial(adam_kernel, start, width, len(previous)),
                out_shape=[shape((rows, 4 * width), BF16), shape((rows, total), BF16)],
                in_specs=[SMEM, SMEM] + [VMEM] * 4 + [HBM] * (3 + len(previous)),
                out_specs=[VMEM, HBM],
                scratch_shapes=[pltpu.VMEM((rows, 4 * width), BF16)] * 4
                + [pltpu.SemaphoreType.DMA((4,))],
                input_output_aliases={9: 1} if previous else {},
                compiler_params=params_of(),
        cost_estimate=LIGHT,
            )(place, bias, *grads, params, first, second, *previous)
        with jax.named_scope("average"):
            received = gossip(stepped, offset, which)
            history.append((codes[0], grads[2], received))
            previous = [] if averaged is None else [averaged]
            averaged = pl.pallas_call(
                functools.partial(average_kernel, start, len(previous)),
                out_shape=shape((rows, total), BF16),
                in_specs=[VMEM, VMEM] + [HBM] * len(previous),
                out_specs=HBM,
                scratch_shapes=[pltpu.VMEM((rows, 4 * width), BF16), pltpu.SemaphoreType.DMA],
                input_output_aliases={2: 0} if previous else {},
                compiler_params=params_of(),
        cost_estimate=LIGHT,
            )(stepped, received, *previous)
    return averaged, moment


def per_device(
    activations, out_grads, params, first_moment, second_moment, gossip_round, step_count
):
    index = lax.axis_index("shard")
    place = jnp.stack([index // 4, index // 2 % 2, index % 2]).astype(jnp.int32)
    count_float = step_count[0].astype(F32)
    bias_one = 1.0 - jnp.power(F32(0.9), count_float)
    bias_two = 1.0 - jnp.power(F32(0.999), count_float)
    bias = jnp.stack([1.0 / bias_one, 1.0 / bias_two])
    operands = (
        activations[0],
        out_grads[0],
        params[0],
        first_moment[0],
        second_moment[0],
        place,
        bias,
        gossip_round[0],
    )
    if BRANCHED:
        averaged, moment = lax.cond(
            gossip_round[0] == 0,
            functools.partial(body, 1),
            lambda *rest: lax.cond(
                gossip_round[0] == 2, functools.partial(body, 4), functools.partial(body, 2), *rest
            ),
            *operands,
        )
    else:
        averaged, moment = body(None, *operands)
    return averaged[None], moment[None]


def solution(mesh):
    spec = P("gossip", "shard", None)
    return jax.shard_map(
        per_device,
        mesh=mesh,
        in_specs=(spec,) * 5 + (P(), P()),
        out_specs=(spec, spec),
        check_vma=False,
    )
```

```python
import functools
import math

import jax
import jax.numpy as jnp
from jax import lax
from jax.experimental import pallas as pl
from jax.experimental.pallas import tpu as pltpu
from jax.sharding import PartitionSpec as P

ROUNDS = 3
LANES = 128
BRANCHED = True
WIDTHS = (4, 6, 4)
BF16 = jnp.bfloat16
F32 = jnp.float32
LIGHT = pl.CostEstimate(flops=1, bytes_accessed=1, transcendentals=0)
VMEM_LIMIT = 48 * 1024 * 1024

UNIT = 2.0**-12
CODE = 32767.0 / math.log1p(2.0**11 / UNIT)


def encode(g):
    level = jnp.log(1.0 + jnp.abs(g) * (1.0 / UNIT)) * CODE
    level = jnp.minimum(jnp.floor(level + 0.5), 32767.0)
    return jnp.where(g < 0.0, -level, level).astype(jnp.int32).astype(jnp.int16)


def decode(q):
    level = q.astype(jnp.int32).astype(F32)
    size = (jnp.exp(jnp.abs(level) * (1.0 / CODE)) - 1.0) * UNIT
    return jnp.where(level < 0.0, -size, size)


def chunks(total):
    out, at = [], 0
    for i, tiles in enumerate(WIDTHS):
        width = tiles * LANES
        if i == len(WIDTHS) - 1:
            at = total - 4 * width
        out.append((at, width))
        at += 4 * width
    return out


def params_of(**kw):
    return pltpu.CompilerParams(vmem_limit_bytes=VMEM_LIMIT, **kw)


SMEM = pl.BlockSpec(memory_space=pltpu.SMEM)
VMEM = pl.BlockSpec(memory_space=pltpu.VMEM)
HBM = pl.BlockSpec(memory_space=pl.ANY)


def cols(start, width):
    return pl.ds(pl.multiple_of(start, LANES), width)


def first_kernel(plan, place, act, dy, a0, a1, a2, a3, csend):
    y, c = place[0], place[2]
    rows = a0.shape[0]
    for r, out in enumerate((a0, a1, a2, a3)):
        quarter = lax.rem(y + r, 4)
        out[...] = act[:, cols(quarter * rows, rows)].T
    at = 0
    for start, width in plan:
        for x in range(2):
            csend[:, at : at + width] = dy[:, cols(start + (x * 2 + 1 - c) * width, width)]
            at += width


def split_kernel(start, width, at, place, dy, crecv, *rest):
    near, far = rest[-2:]
    x, c = place[1], place[2]
    tokens = dy.shape[0]
    for side, out in ((x, near), (1 - x, far)):
        out[:tokens, :] = dy[:, cols(start + (side * 2 + c) * width, width)]
        out[tokens:, :] = crecv[:, cols(at + side * width, width)]


def stack_kernel(p0, p1, p2, p3, *rest):
    out, sems = rest[-2:]
    copies = [
        pltpu.make_async_copy(p, out.at[n], sems.at[n]) for n, p in enumerate((p0, p1, p2, p3))
    ]
    for copy in copies:
        copy.start()
    for copy in copies:
        copy.wait()


def matmul_kernel(n_order, place, b0, bc, bx, bxc, *rest):
    pieces, rest = rest[:8], rest[8 + n_order :]
    outs = rest[:4]
    lhs, rhs, acc, sems = rest[4:]
    x, c = place[1], place[2]
    quarter, tokens = b0.shape[1], b0.shape[2]
    copies = []
    for i in range(4):
        for k, b in enumerate((b0, bc, bx, bxc)):
            copies.append((b.at[i], lhs.at[:, (i * 4 + k) * tokens : (i * 4 + k + 1) * tokens]))
        for k in range(2):
            p = pieces[2 * i + k]
            depth = 2 * tokens
            copies.append((p, rhs.at[(2 * i + k) * depth : (2 * i + k + 1) * depth]))
    copies = [pltpu.make_async_copy(s, d, sems.at[n]) for n, (s, d) in enumerate(copies)]
    for copy in copies:
        copy.start()
    for copy in copies:
        copy.wait()
    width = rhs.shape[1]
    part = 256 if width % 256 == 0 else LANES

    def columns(n, _):
        where = cols(n * part, part)
        acc[:, where] = jnp.dot(lhs[...], rhs[:, where], preferred_element_type=F32)
        return 0

    lax.fori_loop(0, width // part, columns, 0)
    rows = quarter // 4
    step = 16
    for k, out in enumerate(outs):
        dx, dc = k // 2, k % 2
        xx = x if dx == 0 else 1 - x
        cc = c if dc == 0 else 1 - c
        base = (xx * 2 + cc) * rows

        def some(i, _, base=base, out=out):
            r = pl.ds(pl.multiple_of(i * step, step), step)
            out[r, :] = encode(acc[pl.ds(pl.multiple_of(base + i * step, step), step), :])
            return 0

        lax.fori_loop(0, rows // step, some, 0)


def adam_kernel(start, width, n_prev, place, bias, *rest):
    g = rest[:4]
    params, first, second = rest[4:7]
    rest = rest[7 + n_prev :]
    stepped, moment, pv, fv, sv, mv, sems = rest
    x, c = place[1], place[2]
    rows = stepped.shape[0]
    window = pl.ds(start, 4 * width)
    loads = [
        pltpu.make_async_copy(src.at[:, window], dst, sems.at[n])
        for n, (src, dst) in enumerate(((params, pv), (first, fv), (second, sv)))
    ]
    for copy in loads:
        copy.start()
    for copy in loads:
        copy.wait()
    inv_one, inv_two = bias[0], bias[1]
    step = 16
    for k in range(4):
        dx, dc = k // 2, k % 2
        xx = x if dx == 0 else 1 - x
        cc = c if dc == 0 else 1 - c
        where = cols((xx * 2 + cc) * width, width)

        def body(i, _, k=k, where=where):
            r = pl.ds(pl.multiple_of(i * step, step), step)
            grad = decode(g[k][r, :])
            one = 0.9 * fv[r, where].astype(F32) + 0.1 * grad
            two = 0.999 * sv[r, where].astype(F32) + 0.001 * grad * grad
            update = (one * inv_one) / (jnp.sqrt(two * inv_two) + 1e-08)
            new = pv[r, where].astype(F32) * (1.0 - 0.02 * 0.1) - 0.02 * update
            stepped[r, where] = new.astype(BF16)
            mv[r, where] = one.astype(BF16)
            return 0

        lax.fori_loop(0, rows // step, body, 0)
    out = pltpu.make_async_copy(mv, moment.at[:, window], sems.at[3])
    out.start()
    out.wait()


def average_kernel(start, n_prev, own, other, *rest):
    averaged, buf, sem = rest[n_prev:]
    buf[...] = (0.5 * (own[...].astype(F32) + other[...].astype(F32))).astype(BF16)
    out = pltpu.make_async_copy(buf, averaged.at[:, pl.ds(start, buf.shape[1])], sem)
    out.start()
    out.wait()


def moved(block, dy=0, dx=0, dc=0):
    route = []
    for i in range(16):
        y, x, c = i // 4, i // 2 % 2, i % 2
        route.append((i, ((y + dy) % 4 * 2 + (x + dx) % 2) * 2 + (c + dc) % 2))
    return lax.ppermute(block, "shard", route)


def gossip(block, offset, which):
    if offset is None:
        shifts = [functools.partial(gossip, offset=2**k, which=which) for k in range(ROUNDS)]
        return lax.switch(which, shifts, block)
    return lax.ppermute(block, "gossip", [(i, (i + offset) % 16) for i in range(16)])


def body(offset, act, dy, params, first, second, place, bias, which):
    tokens, depth = act.shape
    total = dy.shape[1]
    rows = params.shape[0]
    quarter = depth // 4
    plan = chunks(total)
    half = sum(2 * w for _, w in plan)
    shape = jax.ShapeDtypeStruct
    with jax.named_scope("arrange"):
        a0, a1, a2, a3, csend = pl.pallas_call(
            functools.partial(first_kernel, plan),
            out_shape=[shape((quarter, tokens), BF16)] * 4 + [shape((tokens, half), BF16)],
            in_specs=[SMEM, VMEM, VMEM],
            out_specs=[VMEM] * 5,
            compiler_params=params_of(),
        cost_estimate=LIGHT,
        )(place, act, dy)
        crecv = moved(csend, dc=1)

    def split(j, at, order):
        start, width = plan[j]
        with jax.named_scope("arrange"):
            return pl.pallas_call(
                functools.partial(split_kernel, start, width, at),
                out_shape=[shape((2 * tokens, width), BF16)] * 2,
                in_specs=[SMEM, VMEM, VMEM] + [HBM] * len(order),
                out_specs=[VMEM] * 2,
                compiler_params=params_of(),
        cost_estimate=LIGHT,
            )(place, dy, crecv, *order)

    splits = [sum(2 * w for _, w in plan[:j]) for j in range(len(plan))]
    near, far_out = [None] * len(plan), [None] * len(plan)
    far = [None] * len(plan)

    def send(j, order):
        near[j], far_out[j] = split(j, splits[j], order)
        with jax.named_scope("gather"):
            far[j] = moved(far_out[j], dx=1)

    ring = {}

    def circulate(j):
        with jax.named_scope("gather"):
            own_l, own_r = moved(near[j], dy=1), moved(near[j], dy=3)
            far_r, far_l = moved(far[j], dy=3), moved(far[j], dy=1)
            own_o, far_o = moved(own_l, dy=1), moved(far_r, dy=3)
        ring[j] = (near[j], far[j], own_l, far_l, own_r, far_r, own_o, far_o)

    send(0, [])
    send(1, [far[0]])
    circulate(0)
    circulate(1)
    with jax.named_scope("activations"):
        order = [far[0]]
        b0 = pl.pallas_call(
            stack_kernel,
            out_shape=shape((4, quarter, tokens), BF16),
            in_specs=[HBM] * (4 + len(order)),
            out_specs=HBM,
            scratch_shapes=[pltpu.SemaphoreType.DMA((4,))],
            compiler_params=params_of(),
            cost_estimate=LIGHT,
        )(a0, moved(a1, dy=1), moved(a3, dy=3), moved(a2, dy=2), *order)
        bc = moved(b0, dc=1)
        bx = moved(b0, dx=1)
        bxc = moved(bx, dc=1)
    if len(plan) > 2:
        send(2, [bx, ring[1][2]])
        circulate(2)

    moment = averaged = None
    history = []
    for j, (start, width) in enumerate(plan):
        if j > 2:
            send(j, [history[j - 3][0]])
            circulate(j)
        pieces = ring[j]
        order = [far[2]] if j == 0 and len(plan) > 2 else []
        if j > 0:
            order.append(history[j - 1][1])
        if j > 1:
            order.append(history[j - 2][2])
        if j > 0 and j + 1 in ring:
            order.append(ring[j + 1][2])
        with jax.named_scope("gradient"):
            codes = pl.pallas_call(
                functools.partial(matmul_kernel, len(order)),
                out_shape=[shape((rows, width), jnp.int16)] * 4,
                in_specs=[SMEM] + [HBM] * (12 + len(order)),
                out_specs=[VMEM] * 4,
                scratch_shapes=[
                    pltpu.VMEM((quarter, 16 * tokens), BF16),
                    pltpu.VMEM((16 * tokens, width), BF16),
                    pltpu.VMEM((quarter, width), F32),
                    pltpu.SemaphoreType.DMA((24,)),
                ],
                compiler_params=params_of(),
        cost_estimate=LIGHT,
            )(place, b0, bc, bx, bxc, *pieces, *order)
            grads = [
                codes[0],
                moved(codes[1], dc=1),
                moved(codes[2], dx=1),
                moved(codes[3], dx=1, dc=1),
            ]
        with jax.named_scope("adam"):
            previous = [] if moment is None else [moment]
            stepped, moment = pl.pallas_call(
                functools.partial(adam_kernel, start, width, len(previous)),
                out_shape=[shape((rows, 4 * width), BF16), shape((rows, total), BF16)],
                in_specs=[SMEM, SMEM] + [VMEM] * 4 + [HBM] * (3 + len(previous)),
                out_specs=[VMEM, HBM],
                scratch_shapes=[pltpu.VMEM((rows, 4 * width), BF16)] * 4
                + [pltpu.SemaphoreType.DMA((4,))],
                input_output_aliases={9: 1} if previous else {},
                compiler_params=params_of(),
        cost_estimate=LIGHT,
            )(place, bias, *grads, params, first, second, *previous)
        with jax.named_scope("average"):
            received = gossip(stepped, offset, which)
            history.append((codes[0], grads[2], received))
            previous = [] if averaged is None else [averaged]
            averaged = pl.pallas_call(
                functools.partial(average_kernel, start, len(previous)),
                out_shape=shape((rows, total), BF16),
                in_specs=[VMEM, VMEM] + [HBM] * len(previous),
                out_specs=HBM,
                scratch_shapes=[pltpu.VMEM((rows, 4 * width), BF16), pltpu.SemaphoreType.DMA],
                input_output_aliases={2: 0} if previous else {},
                compiler_params=params_of(),
        cost_estimate=LIGHT,
            )(stepped, received, *previous)
    return averaged, moment


def per_device(
    activations, out_grads, params, first_moment, second_moment, gossip_round, step_count
):
    index = lax.axis_index("shard")
    place = jnp.stack([index // 4, index // 2 % 2, index % 2]).astype(jnp.int32)
    count_float = step_count[0].astype(F32)
    bias_one = 1.0 - jnp.power(F32(0.9), count_float)
    bias_two = 1.0 - jnp.power(F32(0.999), count_float)
    bias = jnp.stack([1.0 / bias_one, 1.0 / bias_two])
    operands = (
        activations[0],
        out_grads[0],
        params[0],
        first_moment[0],
        second_moment[0],
        place,
        bias,
        gossip_round[0],
    )
    if BRANCHED:
        averaged, moment = lax.cond(
            gossip_round[0] == 0,
            functools.partial(body, 1),
            lambda *rest: lax.cond(
                gossip_round[0] == 2, functools.partial(body, 4), functools.partial(body, 2), *rest
            ),
            *operands,
        )
    else:
        averaged, moment = body(None, *operands)
    return averaged[None], moment[None]


def solution(mesh):
    spec = P("gossip", "shard", None)
    return jax.shard_map(
        per_device,
        mesh=mesh,
        in_specs=(spec,) * 5 + (P(), P()),
        out_specs=(spec, spec),
        check_vma=False,
    )
```
